512 devices in a mesh: dp: 32 (over z, core), fsdp: 16 (over x, y).
Axes of the slice: x: 4, y: 4, z: 16, core: 2. Of those that a mesh axis runs over, the one named last changes fastest.
Arguments:
- token_ids: int32 [65536], P(('dp', 'fsdp')), may hold values from 0 to 50431, as said below
- activations: bfloat16 [65536, 3072], P(('dp', 'fsdp'))
- grad_out: bfloat16 [65536, 3072], P(('dp', 'fsdp')), may hold values from -0.13183594 to 0.13183594
- error_buffer: bfloat16 [32, 3072, 3072], P('dp', 'fsdp'), may hold values from -6 to 6
- init_q: float32 [3072, 8], replicated, may hold values from -6 to 6
Outputs:
- p_factor: float32 [3072, 8], P('fsdp')
- q_factor: float32 [3072, 8], replicated
- error_next: bfloat16 [32, 3072, 3072], P('dp', 'fsdp')
The draws below stay inside these ranges and needn't reach their ends.
Inputs may be any that keep to these rules, and one draw needn't show every extreme that they name: `token_ids`: id 1 is padding; on the rows of each device it forms a tail (possibly empty), and each device's first row holds id 0.
All inputs are finite; a program needn't handle non-finite values.
Results may differ from the reference program's by a relative error of at most 0.0006.
Values may be sent and summed in bfloat16 or wider, within the bound.
No kernel may reach another device: no remote copies, remote signals or barrier semaphores. Data moves between devices by JAX's collectives and lax.ppermute only.
A program may use at most 64 MiB of HBM per device.

```python
import math
import jax
import jax.numpy as jnp
from jax import lax

VOCAB = 50432
DIN = 3072
DOUT = 3072
RANK = 8
TOK_DEV = 128
TOKENS = 65536
N_DP = 32
N_FSDP = 16


def draw_token_ids(key, part):
    key = jax.random.fold_in(key, 11)
    key_len, key_ids = jax.random.split(key)
    blocks = TOKENS // TOK_DEV
    lowest = max(TOK_DEV // 4, 1)
    lengths = jax.random.randint(key_len, (blocks, 1), lowest, TOK_DEV + 1)
    block_index = jnp.arange(blocks)[:, None]
    lengths = jnp.where(block_index == 0, TOK_DEV, lengths)
    drawn_ids = jax.random.randint(key_ids, (blocks, TOK_DEV), 2, VOCAB)
    position = jnp.arange(TOK_DEV)[None, :]
    drawn_ids = jnp.where(position < lengths, drawn_ids, 1)
    drawn_ids = jnp.where((block_index == 0) & (position == 1), VOCAB - 1, drawn_ids)
    drawn_ids = jnp.where(position == 0, 0, drawn_ids)
    return drawn_ids.reshape(TOKENS).astype(jnp.int32)


def draw_activations(key, part):
    key = jax.random.fold_in(key, 23)
    key_main = jax.random.fold_in(key, 0)
    column = jnp.arange(DIN, dtype=jnp.float32) / max(DIN - 1, 1)
    scales = jnp.exp(column * math.log(10.0))
    noise = jnp.clip(jax.random.normal(key_main, (TOKENS, DIN), jnp.float32), -6.0, 6.0)
    values = scales[None, :] * noise
    return values.astype(jnp.bfloat16)


def block_scale(key, extent, pieces, smallest, largest):
    def one(dim, shards_of):
        steps = jax.random.uniform(jax.random.fold_in(jax.random.fold_in(key, 6), dim), (shards_of,), jnp.float32, smallest / len(pieces), largest / len(pieces))
        return jnp.repeat(jnp.exp(steps), extent[dim] // shards_of).reshape((-1,) + (1,) * (len(extent) - dim - 1))

    factor_of = one(*pieces[0])
    for cut in pieces[1:]:
        factor_of = factor_of * one(*cut)
    return factor_of


def centred(rng, extent, spread, bound, shards=(), kind=jnp.bfloat16):
    array = jax.random.normal(rng, extent, jnp.float32) * spread
    if len(shards) > 0:
        array = block_scale(rng, extent, shards, -0.22, 0.18) * array
    return jnp.clip(array, min=-bound, max=bound).astype(kind)


def setup_inputs(seed: int = 0) -> dict:
    key_list = jax.random.split(jax.random.key(seed), 6)
    return {
        "token_ids": draw_token_ids(jax.random.fold_in(key_list[5], 71), 0),
        "activations": draw_activations(jax.random.fold_in(key_list[5], 71), 0),
        "grad_out": centred(key_list[2], (TOKENS, DOUT), (1.0 / (TOK_DEV * N_FSDP) ** 0.5), 0.13183594, ((0, 512),)),
        "error_buffer": centred(key_list[3], (N_DP, DIN, DOUT), 1.0, 6.0, ((0, 32), (1, 16))),
        "init_q": centred(key_list[4], (DOUT, RANK), 1.0, 6.0, (), jnp.float32),
    }


def replica_merge(operands):
    token_block, grad_block, error_block = operands
    product = jnp.dot(token_block.T.astype(jnp.float32), grad_block.astype(jnp.float32), preferred_element_type=jnp.float32)
    return product + error_block.astype(jnp.float32)

def reference(token_ids, activations, grad_out, error_buffer, init_q):
    highest = lax.Precision.HIGHEST
    valid_rows = (token_ids != 1).astype(grad_out.dtype)
    masked_grad = grad_out * valid_rows[:, None]
    token_blocks = activations.reshape(N_DP, -1, DIN)
    grad_blocks = masked_grad.reshape(N_DP, -1, DOUT)
    merged = lax.map(replica_merge, (token_blocks, grad_blocks, error_buffer))
    p_mean = jnp.einsum('rij,jk->ik', merged, init_q.astype(jnp.float32), precision=highest) / N_DP
    gram_matrix = jnp.dot(p_mean.T, p_mean, precision=highest)
    factor_low = jnp.linalg.cholesky(gram_matrix)
    p_factor = jax.scipy.linalg.solve_triangular(factor_low, p_mean.T, lower=True).T
    q_factor = jnp.einsum('rij,ik->jk', merged, p_factor, precision=highest) / N_DP
    error_next = (merged - jnp.dot(p_factor, q_factor.T, precision=highest)[None]).astype(jnp.bfloat16)
    return (p_factor, q_factor, error_next)
```

```python
import math

import jax
import jax.numpy as jnp
from jax import lax
from jax.experimental import pallas as pl
from jax.experimental.pallas import tpu as pltpu
from jax.sharding import Mesh, PartitionSpec as P

RANK = 8
F32, BF16 = jnp.float32, jnp.bfloat16
ROWS_OF_SPLIT = 4 * RANK
NT = (((1,), (1,)), ((), ()))
TN = (((0,), (0,)), ((), ()))
XP_SCALE = 2.0**-8


def terms(value):
    high = value.astype(BF16).astype(F32)
    rest = value - high
    middle = rest.astype(BF16).astype(F32)
    return high, middle, rest - middle


def split(value):
    return jnp.concatenate([*terms(value), jnp.zeros_like(value)], axis=0).astype(BF16)


def join(value):
    return value[:RANK] + value[RANK : 2 * RANK] + value[2 * RANK : 3 * RANK]


def dot(a, b, dims=(((1,), (0,)), ((), ()))):
    return lax.dot_general(a, b, dims, preferred_element_type=F32)


def lanes(ref, rows=slice(None)):
    return jnp.concatenate([ref[i, rows, :] for i in range(ref.shape[0])], axis=1)


def call(kernel, out_shape, *args, flops=0):
    nbytes = sum(math.prod(a.shape) * a.dtype.itemsize for a in args)
    return pl.pallas_call(
        kernel,
        out_shape=out_shape,
        in_specs=[pl.BlockSpec(memory_space=pltpu.VMEM)] * len(args),
        out_specs=jax.tree.map(lambda _: pl.BlockSpec(memory_space=pltpu.VMEM), out_shape),
        compiler_params=pltpu.CompilerParams(vmem_limit_bytes=40 * 2**20),
        cost_estimate=pl.CostEstimate(flops=flops, bytes_accessed=nbytes, transcendentals=0),
    )(*args)


def pack_kernel(ids_ref, x_ref, g_ref, initq_ref, pay_ref):
    parts, rows, _ = pay_ref.shape
    width = rows - ROWS_OF_SPLIT
    valid = (ids_ref[...] != 1).astype(F32)
    gq = join(dot(split(initq_ref[...]), g_ref[...], NT))
    gq = split(gq * valid)
    for i in range(parts):
        block = x_ref[:, i * width : (i + 1) * width].astype(F32).T * valid
        pay_ref[i, :width, :] = block.astype(BF16)
        pay_ref[i, width:, :] = gq


def left_kernel(recv_ref, e_ref, initq_ref, p_ref):
    width = recv_ref.shape[1] - ROWS_OF_SPLIT
    x_cols = lanes(recv_ref, slice(0, width))
    gq = lanes(recv_ref, slice(width, None))
    p_ref[...] = join(dot(gq, x_cols, NT)) + join(dot(split(initq_ref[...]), e_ref[...], NT))


def inverse_factor(gram):
    eye = (lax.broadcasted_iota(jnp.int32, gram.shape, 0) == lax.broadcasted_iota(jnp.int32, gram.shape, 1)).astype(F32)
    row = lax.broadcasted_iota(jnp.int32, (RANK, 1), 0)
    left, right = gram, eye
    scale = jnp.zeros((RANK, 1), F32)
    for k in range(RANK):
        pivot = left[k : k + 1, k : k + 1]
        factor = jnp.where(row > k, left[:, k : k + 1] / pivot, 0.0)
        scale = jnp.where(row == k, lax.rsqrt(pivot), scale)
        next_left = left - factor * left[k : k + 1, :]
        right = right - factor * right[k : k + 1, :]
        left = next_left
    return right * scale


def right_kernel(pfull_ref, pown_ref, pay_ref, g_ref, e_ref, pout_ref, q_ref):
    parts, _, width = pfull_ref.shape
    high = dict(precision=lax.Precision.HIGHEST, preferred_element_type=F32)
    p_full = lanes(pfull_ref)
    gram = lax.dot_general(p_full, p_full, NT, **high)
    inverse = inverse_factor(gram)
    factor = jnp.dot(inverse, p_full, **high)
    own = jnp.dot(inverse, pown_ref[...], **high)
    pout_ref[...] = own
    small = split(factor * XP_SCALE)
    x_rows = jnp.concatenate([pay_ref[i, :width, :] for i in range(parts)], axis=0)
    xp = split(join(dot(small, x_rows)))
    q = join(dot(xp, g_ref[...])) * (1.0 / XP_SCALE) + join(dot(split(own), e_ref[...]))
    for i in range(parts):
        q_ref[i] = q[:, i * width : (i + 1) * width]


def final_kernel(recv_ref, g_ref, e_ref, p_ref, q_ref, out_ref):
    width = recv_ref.shape[1] - ROWS_OF_SPLIT
    p_high, p_middle, p_low = terms(p_ref[...])
    q_high, q_middle, q_low = terms(q_ref[...])
    p_terms = jnp.concatenate([p_high, p_high, p_middle, p_high, p_low, p_middle], axis=0).astype(BF16)
    q_terms = jnp.concatenate([q_high, q_middle, q_high, q_low, q_high, q_middle], axis=0).astype(BF16)
    merged = dot(lanes(recv_ref, slice(0, width)), g_ref[...]) + e_ref[...].astype(F32)
    out_ref[...] = (merged - dot(p_terms, q_terms, TN)).astype(BF16)


def final(recv, g_all, error_rows, p_own, q_full):
    parts, rows, tokens = recv.shape
    width, columns = error_rows.shape
    tile = math.gcd(columns, 384)
    return pl.pallas_call(
        final_kernel,
        out_shape=jax.ShapeDtypeStruct((width, columns), BF16),
        grid=(columns // tile,),
        in_specs=[
            pl.BlockSpec((parts, rows, tokens), lambda j: (0, 0, 0)),
            pl.BlockSpec((parts * tokens, tile), lambda j: (0, j)),
            pl.BlockSpec((width, tile), lambda j: (0, j)),
            pl.BlockSpec((RANK, width), lambda j: (0, 0)),
            pl.BlockSpec((RANK, tile), lambda j: (0, j)),
        ],
        out_specs=pl.BlockSpec((width, tile), lambda j: (0, j)),
        compiler_params=pltpu.CompilerParams(vmem_limit_bytes=40 * 2**20),
        cost_estimate=pl.CostEstimate(
            flops=2 * width * columns * parts * tokens,
            bytes_accessed=2 * columns * (parts * tokens + 2 * width),
            transcendentals=0,
        ),
    )(recv, g_all, error_rows, p_own, q_full)


def exchange(value, axes):
    return lax.all_to_all(value, axes, split_axis=0, concat_axis=0, tiled=True)


def gather(value, axes, parts):
    return exchange(jnp.broadcast_to(value[None], (parts, *value.shape)), axes)


def on_device(token_ids, activations, grad_out, error_buffer, init_q):
    plane = ("x", "y")
    parts = lax.axis_size(plane)
    depth = lax.axis_size("z")
    replicas = depth * lax.axis_size("core")
    tokens, features = activations.shape
    width = features // parts
    columns = grad_out.shape[1]
    error_rows = error_buffer[0]
    initq_t = init_q.T

    def over_replicas(value):
        return jnp.sum(gather(lax.psum(value, "core"), "z", depth), axis=0) / replicas

    g_all = lax.all_gather(grad_out, plane, axis=0, tiled=True)
    payload = call(
        pack_kernel,
        jax.ShapeDtypeStruct((parts, width + ROWS_OF_SPLIT, tokens), BF16),
        token_ids[None], activations, grad_out, initq_t,
    )
    recv = exchange(payload, plane)
    p_local = call(left_kernel, jax.ShapeDtypeStruct((RANK, width), F32), recv, error_rows, initq_t)
    p_mean = over_replicas(p_local)
    p_full = gather(p_mean, plane, parts)
    p_own, q_terms = call(
        right_kernel,
        (
            jax.ShapeDtypeStruct((RANK, width), F32),
            jax.ShapeDtypeStruct((parts, RANK, columns // parts), F32),
        ),
        p_full, p_mean, payload, grad_out, error_rows,
    )
    q_own = over_replicas(jnp.sum(exchange(q_terms, plane), axis=0))
    q_full = gather(q_own, plane, parts).swapaxes(0, 1).reshape(RANK, columns)
    error_next = final(recv, g_all, error_rows, p_own, q_full)
    return p_own.T, q_full.T, error_next[None]


def solution(mesh):
    replicas, parts = mesh.shape["dp"], mesh.shape["fsdp"]
    side = math.isqrt(parts)
    fine = Mesh(mesh.devices.reshape(replicas // 2, 2, side, parts // side), ("z", "core", "x", "y"))
    everywhere = ("z", "core", "x", "y")
    return jax.shard_map(
        on_device,
        mesh=fine,
        in_specs=(
            P(everywhere),
            P(everywhere, None),
            P(everywhere, None),
            P(("z", "core"), ("x", "y"), None),
            P(),
        ),
        out_specs=(P(("x", "y"), None), P(), P(("z", "core"), ("x", "y"), None)),
        check_vma=False,
    )
```

```python
import functools
import math

import jax
import jax.numpy as jnp
from jax import lax
from jax.experimental import pallas as pl
from jax.experimental.pallas import tpu as pltpu
from jax.sharding import Mesh, PartitionSpec as P

RANK = 8
LANES = 128
SPLIT_ROWS = 4 * RANK
F32, BF16 = jnp.float32, jnp.bfloat16
NT = (((1,), (1,)), ((), ()))
TN = (((0,), (0,)), ((), ()))
XP_SCALE = 2.0**-8
VMEM = pl.BlockSpec(memory_space=pltpu.VMEM)
ANY = pl.BlockSpec(memory_space=pl.ANY)


def terms(value):
    high = value.astype(BF16).astype(F32)
    rest = value - high
    middle = rest.astype(BF16).astype(F32)
    return high, middle, rest - middle


def split(value):
    return jnp.concatenate([*terms(value), jnp.zeros_like(value)], axis=0).astype(BF16)


def join(value):
    return value[:RANK] + value[RANK : 2 * RANK] + value[2 * RANK : 3 * RANK]


def dot(a, b, dims=(((1,), (0,)), ((), ()))):
    return lax.dot_general(a, b, dims, preferred_element_type=F32)


def stack(value):
    return jnp.concatenate([value[:, i : i + LANES] for i in range(0, value.shape[1], LANES)], axis=0)


def unstack(value):
    return jnp.concatenate([value[i : i + RANK] for i in range(0, value.shape[0], RANK)], axis=1)


def lanes(ref, rows=slice(None)):
    return jnp.concatenate([ref[i, rows, :] for i in range(ref.shape[0])], axis=1)


def call(kernel, out_shape, specs, *args, scratch=(), flops=0):
    nbytes = sum(math.prod(a.shape) * a.dtype.itemsize for a in args)
    return pl.pallas_call(
        kernel,
        out_shape=out_shape,
        in_specs=specs,
        out_specs=jax.tree.map(lambda _: VMEM, out_shape),
        scratch_shapes=scratch,
        compiler_params=pltpu.CompilerParams(vmem_limit_bytes=40 * 2**20),
        cost_estimate=pl.CostEstimate(flops=flops, bytes_accessed=nbytes, transcendentals=0),
    )(*args)


def pack_kernel(ids_hbm, x_hbm, g_hbm, initq_hbm, pay_ref, ids_ref, x_ref, g_ref, initq_ref, sems):
    sources = (initq_hbm, g_hbm, ids_hbm, x_hbm)
    targets = (initq_ref, g_ref, ids_ref, x_ref)
    copies = [pltpu.make_async_copy(*pair, sems.at[i]) for i, pair in enumerate(zip(sources, targets))]
    for copy in copies:
        copy.start()
    for copy in copies[:3]:
        copy.wait()
    parts, rows, _ = pay_ref.shape
    width = rows - SPLIT_ROWS
    valid = (ids_ref[...] != 1).astype(F32)
    gq = split(join(dot(split(initq_ref[...]), g_ref[...], NT)) * valid)
    copies[3].wait()
    for i in range(parts):
        block = x_ref[:, i * width : (i + 1) * width].astype(F32).T * valid
        pay_ref[i, :width, :] = block.astype(BF16)
        pay_ref[i, width:, :] = gq


def left_kernel(recv_ref, e_ref, initq_ref, p_ref):
    width = recv_ref.shape[1] - SPLIT_ROWS
    x_cols = lanes(recv_ref, slice(0, width))
    gq = lanes(recv_ref, slice(width, None))
    p_ref[...] = join(dot(gq, x_cols, NT)) + join(dot(split(initq_ref[...]), e_ref[...], NT))


def inverse_factor(gram):
    eye = (lax.broadcasted_iota(jnp.int32, gram.shape, 0) == lax.broadcasted_iota(jnp.int32, gram.shape, 1)).astype(F32)
    row = lax.broadcasted_iota(jnp.int32, (RANK, 1), 0)
    left, right = gram, eye
    scale = jnp.zeros((RANK, 1), F32)
    for k in range(RANK):
        pivot = left[k : k + 1, k : k + 1]
        factor = jnp.where(row > k, left[:, k : k + 1] / pivot, 0.0)
        scale = jnp.where(row == k, lax.rsqrt(pivot), scale)
        next_left = left - factor * left[k : k + 1, :]
        right = right - factor * right[k : k + 1, :]
        left = next_left
    return right * scale


def right_kernel(pfull_ref, pown_ref, ids_ref, x_ref, g_ref, e_ref, own_ref, q_ref):
    high = dict(precision=lax.Precision.HIGHEST, preferred_element_type=F32)
    p_full = lanes(pfull_ref)
    gram = lax.dot_general(p_full, p_full, NT, **high)
    inverse = inverse_factor(gram)
    factor = jnp.dot(inverse, p_full, **high)
    own = jnp.dot(inverse, pown_ref[...], **high)
    own_ref[...] = own
    valid = ids_ref[...] != 1
    xp = join(dot(split(factor * XP_SCALE), x_ref[...], NT))
    xp = split(jnp.where(valid, xp, 0.0))
    q = join(dot(xp, g_ref[...])) * (1.0 / XP_SCALE) + join(dot(split(own), e_ref[...]))
    q_ref[...] = stack(q)


def final_kernel(replicas, recv_ref, g_ref, e_ref, p_ref, q_ref, out_ref, qout_ref):
    width = out_ref.shape[0]
    q = unstack(q_ref[...]) * (1.0 / replicas)
    qout_ref[...] = q
    p_high, p_middle, p_low = terms(p_ref[...])
    q_high, q_middle, q_low = terms(q)
    p_terms = jnp.concatenate([p_high, p_high, p_middle, p_high, p_low, p_middle], axis=0).astype(BF16)
    q_terms = jnp.concatenate([q_high, q_middle, q_high, q_low, q_high, q_middle], axis=0).astype(BF16)
    merged = dot(lanes(recv_ref, slice(0, width)), g_ref[...]) + e_ref[...].astype(F32)
    out_ref[...] = (merged - dot(p_terms, q_terms, TN)).astype(BF16)


def final(replicas, recv, g_all, error_rows, p_own, q_sum):
    parts, _, tokens = recv.shape
    width, columns = error_rows.shape
    tile = math.gcd(columns, 768)
    return pl.pallas_call(
        functools.partial(final_kernel, replicas),
        out_shape=(jax.ShapeDtypeStruct((width, columns), BF16), jax.ShapeDtypeStruct((RANK, columns), F32)),
        grid=(columns // tile,),
        in_specs=[
            pl.BlockSpec(recv.shape, lambda j: (0, 0, 0)),
            pl.BlockSpec((parts * tokens, tile), lambda j: (0, j)),
            pl.BlockSpec((width, tile), lambda j: (0, j)),
            pl.BlockSpec((RANK, width), lambda j: (0, 0)),
            pl.BlockSpec((tile * RANK // LANES, LANES), lambda j: (j, 0)),
        ],
        out_specs=(pl.BlockSpec((width, tile), lambda j: (0, j)), pl.BlockSpec((RANK, tile), lambda j: (0, j))),
        compiler_params=pltpu.CompilerParams(vmem_limit_bytes=40 * 2**20),
        cost_estimate=pl.CostEstimate(
            flops=2 * width * columns * parts * tokens,
            bytes_accessed=2 * columns * (parts * tokens + 2 * width),
            transcendentals=0,
        ),
    )(recv, g_all, error_rows, p_own, q_sum)


def exchange(value, axes):
    return lax.all_to_all(value, axes, split_axis=0, concat_axis=0, tiled=True)


def gather(value, axes, parts):
    return exchange(jnp.broadcast_to(value, (parts, *value.shape[1:])), axes)


def on_device(token_ids, activations, grad_out, error_buffer, init_q):
    plane, near = ("x", "y"), ("core", "x", "y")
    parts, peers, depth = lax.axis_size(plane), lax.axis_size(near), lax.axis_size("z")
    replicas = depth * lax.axis_size("core")
    tokens, features = activations.shape
    width = features // parts
    columns = grad_out.shape[1]
    error_rows = error_buffer[0]
    ids = token_ids[None]
    initq_t = init_q.T

    g_all = lax.all_gather(grad_out, plane, axis=0, tiled=True)
    payload = call(
        pack_kernel,
        jax.ShapeDtypeStruct((parts, width + SPLIT_ROWS, tokens), BF16),
        [ANY] * 4,
        ids, activations, grad_out, initq_t,
        scratch=(
            pltpu.VMEM(ids.shape, ids.dtype),
            pltpu.VMEM(activations.shape, BF16),
            pltpu.VMEM(grad_out.shape, BF16),
            pltpu.VMEM(initq_t.shape, F32),
            pltpu.SemaphoreType.DMA((4,)),
        ),
    )
    recv = exchange(payload, plane)
    p_local = call(left_kernel, jax.ShapeDtypeStruct((RANK, width), F32), [VMEM] * 3, recv, error_rows, initq_t)
    p_mean = jnp.sum(gather(lax.psum(p_local, "core")[None], "z", depth), axis=0) / replicas
    p_full = gather(p_mean[None], plane, parts)
    p_own, q_terms = call(
        right_kernel,
        (
            jax.ShapeDtypeStruct((RANK, width), F32),
            jax.ShapeDtypeStruct((columns * RANK // LANES, LANES), F32),
        ),
        [VMEM] * 6,
        p_full, p_mean, ids, activations, grad_out, error_rows,
    )
    blocks = exchange(q_terms.reshape(peers, 1, q_terms.size // peers), near)
    blocks = gather(jnp.sum(blocks, axis=0, keepdims=True), "z", depth)
    q_sum = gather(jnp.sum(blocks, axis=0, keepdims=True), near, peers).reshape(-1, LANES)
    error_next, q_t = final(replicas, recv, g_all, error_rows, p_own, q_sum)
    return p_own.T, q_t.T, error_next[None]


def solution(mesh):
    replicas, parts = mesh.shape["dp"], mesh.shape["fsdp"]
    side = math.isqrt(parts)
    fine = Mesh(mesh.devices.reshape(replicas // 2, 2, side, parts // side), ("z", "core", "x", "y"))
    everywhere = ("z", "core", "x", "y")
    return jax.shard_map(
        on_device,
        mesh=fine,
        in_specs=(
            P(everywhere),
            P(everywhere, None),
            P(everywhere, None),
            P(("z", "core"), ("x", "y"), None),
            P(),
        ),
        out_specs=(P(("x", "y"), None), P(), P(("z", "core"), ("x", "y"), None)),
        check_vma=False,
    )
```

```python
import functools
import math

import jax
import jax.numpy as jnp
from jax import lax
from jax.experimental import pallas as pl
from jax.experimental.pallas import tpu as pltpu
from jax.sharding import Mesh, PartitionSpec as P

RANK = 8
LANES = 128
SPLIT_ROWS = 2 * RANK
F32, BF16 = jnp.float32, jnp.bfloat16
NT = (((1,), (1,)), ((), ()))
TN = (((0,), (0,)), ((), ()))
XP_SCALE = 2.0**-8
TOKEN_CUTS, COLUMN_CUTS = 8, 2
VMEM = pl.BlockSpec(memory_space=pltpu.VMEM)
HBM = pl.BlockSpec(memory_space=pltpu.HBM)


def terms(value):
    high = value.astype(BF16).astype(F32)
    rest = value - high
    middle = rest.astype(BF16).astype(F32)
    return high, middle, rest - middle


def split(value):
    return jnp.concatenate([*terms(value), jnp.zeros_like(value)], axis=0).astype(BF16)


def join(value):
    return value[:RANK] + value[RANK : 2 * RANK] + value[2 * RANK : 3 * RANK]


def dot(a, b, dims=(((1,), (0,)), ((), ()))):
    return lax.dot_general(a, b, dims, preferred_element_type=F32)


def stack(value):
    return jnp.concatenate([value[:, i : i + LANES] for i in range(0, value.shape[1], LANES)], axis=0)


def unstack(value):
    return jnp.concatenate([value[i : i + RANK] for i in range(0, value.shape[0], RANK)], axis=1)


def lanes(ref, rows=slice(None)):
    return jnp.concatenate([ref[i, rows, :] for i in range(ref.shape[0])], axis=1)


def staged(*arrays):
    return [pltpu.VMEM(a.shape, a.dtype) for a in arrays]


def call(kernel, out_shape, specs, *args, scratch=(), vmem=40):
    nbytes = sum(math.prod(a.shape) * a.dtype.itemsize for a in args)
    return pl.pallas_call(
        kernel,
        out_shape=out_shape,
        in_specs=specs,
        out_specs=jax.tree.map(lambda _: VMEM, out_shape),
        scratch_shapes=scratch,
        compiler_params=pltpu.CompilerParams(vmem_limit_bytes=vmem * 2**20),
        cost_estimate=pl.CostEstimate(flops=0, bytes_accessed=nbytes, transcendentals=0),
    )(*args)


def pack_kernel(ids_hbm, x_hbm, g_hbm, initq_hbm, pay_ref, ids_ref, x_ref, g_ref, initq_ref, sems):
    sources = (initq_hbm, g_hbm, ids_hbm, x_hbm)
    targets = (initq_ref, g_ref, ids_ref, x_ref)
    copies = [pltpu.make_async_copy(*pair, sems.at[i]) for i, pair in enumerate(zip(sources, targets))]
    for copy in copies:
        copy.start()
    for copy in copies[:3]:
        copy.wait()
    parts, rows, _ = pay_ref.shape
    width = rows - SPLIT_ROWS
    valid = (ids_ref[...] != 1).astype(F32)
    gq = join(dot(split(initq_ref[...]), g_ref[...], NT)) * valid
    gq = jnp.concatenate(terms(gq)[:2], axis=0).astype(BF16)
    copies[3].wait()
    for i in range(parts):
        block = x_ref[:, i * width : (i + 1) * width].astype(F32).T * valid
        pay_ref[i, :width, :] = block.astype(BF16)
        pay_ref[i, width:, :] = gq


def left_kernel(recv_ref, e_ref, initq_ref, p_ref):
    width = recv_ref.shape[1] - SPLIT_ROWS
    x_cols = lanes(recv_ref, slice(0, width))
    gq = lanes(recv_ref, slice(width, None))
    p = dot(gq, x_cols, NT)
    p_ref[...] = p[:RANK] + p[RANK:] + join(dot(split(initq_ref[...]), e_ref[...], NT))


def inverse_factor(gram):
    eye = (lax.broadcasted_iota(jnp.int32, gram.shape, 0) == lax.broadcasted_iota(jnp.int32, gram.shape, 1)).astype(F32)
    row = lax.broadcasted_iota(jnp.int32, (RANK, 1), 0)
    left, right = gram, eye
    scale = jnp.zeros((RANK, 1), F32)
    for k in range(RANK):
        pivot = left[k : k + 1, k : k + 1]
        factor = jnp.where(row > k, left[:, k : k + 1] / pivot, 0.0)
        scale = jnp.where(row == k, lax.rsqrt(pivot), scale)
        next_left = left - factor * left[k : k + 1, :]
        right = right - factor * right[k : k + 1, :]
        left = next_left
    return right * scale


def right_kernel(
    pfull_ref, pown_ref, ids_hbm, x_hbm, g_hbm, e_ref, own_ref, again_ref, q_ref, ids_ref, x_ref, g_ref, sems
):
    pairs = ((ids_hbm, ids_ref), (x_hbm, x_ref), (g_hbm, g_ref))
    copies = [pltpu.make_async_copy(*pair, sems.at[i]) for i, pair in enumerate(pairs)]
    for copy in copies:
        copy.start()
    high = dict(precision=lax.Precision.HIGHEST, preferred_element_type=F32)
    p_full = lanes(pfull_ref)
    gram = lax.dot_general(p_full, p_full, NT, **high)
    inverse = inverse_factor(gram)
    factor = jnp.dot(inverse, p_full, **high)
    own = jnp.dot(inverse, pown_ref[...], **high)
    own_ref[...] = own
    again_ref[...] = own
    for copy in copies:
        copy.wait()
    valid = ids_ref[...] != 1
    xp = join(dot(split(factor * XP_SCALE), x_ref[...], NT))
    xp = split(jnp.where(valid, xp, 0.0))
    q = join(dot(xp, g_ref[...])) * (1.0 / XP_SCALE) + join(dot(split(own), e_ref[...]))
    q_ref[...] = stack(q)


def final_kernel(
    replicas, recv_ref, g_hbm, e_ref, p_ref, q_ref, out_hbm, qout_ref, g_ref, total_ref, out_ref, in_sems, out_sems
):
    width, columns = e_ref.shape
    rows, wide = g_hbm.shape[0] // TOKEN_CUTS, columns // COLUMN_CUTS
    spans = [slice(i, i + rows) for i in range(0, g_hbm.shape[0], rows)]
    sides = [slice(j, j + wide) for j in range(0, columns, wide)]
    loads = [pltpu.make_async_copy(g_hbm.at[s], g_ref.at[s], in_sems.at[i]) for i, s in enumerate(spans)]
    stores = [pltpu.make_async_copy(out_ref.at[:, s], out_hbm.at[:, s], out_sems.at[j]) for j, s in enumerate(sides)]
    for load in loads:
        load.start()
    q = unstack(q_ref[...]) * (1.0 / replicas)
    qout_ref[...] = q
    p_high, p_middle, p_low = terms(p_ref[...])
    q_high, q_middle, q_low = terms(q)
    p_terms = jnp.concatenate([p_high, p_high, p_middle, p_high, p_low, p_middle], axis=0).astype(BF16)
    q_terms = jnp.concatenate([q_high, q_middle, q_high, q_low, q_high, q_middle], axis=0).astype(BF16)
    for side in sides:
        total_ref[:, side] = e_ref[:, side].astype(F32) - dot(p_terms, q_terms[:, side], TN)
    x_cols = lanes(recv_ref, slice(0, width))
    for i, span in enumerate(spans):
        loads[i].wait()
        for j, side in enumerate(sides):
            total = total_ref[:, side] + dot(x_cols[:, span], g_ref[span, side])
            if i + 1 < len(spans):
                total_ref[:, side] = total
            else:
                out_ref[:, side] = total.astype(BF16)
                stores[j].start()
    for store in stores:
        store.wait()


def final(replicas, recv, g_all, error_rows, p_own, q_sum):
    width, columns = error_rows.shape
    outs = (jax.ShapeDtypeStruct((width, columns), BF16), jax.ShapeDtypeStruct((RANK, columns), F32))
    return pl.pallas_call(
        functools.partial(final_kernel, replicas),
        out_shape=outs,
        in_specs=[VMEM, HBM, VMEM, VMEM, VMEM],
        out_specs=(HBM, VMEM),
        scratch_shapes=(
            *staged(g_all),
            pltpu.VMEM(error_rows.shape, F32),
            *staged(error_rows),
            pltpu.SemaphoreType.DMA((TOKEN_CUTS,)),
            pltpu.SemaphoreType.DMA((COLUMN_CUTS,)),
        ),
        compiler_params=pltpu.CompilerParams(vmem_limit_bytes=48 * 2**20),
        cost_estimate=pl.CostEstimate(
            flops=2 * width * columns * g_all.shape[0],
            bytes_accessed=2 * columns * (g_all.shape[0] + 2 * width),
            transcendentals=0,
        ),
    )(recv, g_all, error_rows, p_own, q_sum)


def exchange(value, axes):
    return lax.all_to_all(value, axes, split_axis=0, concat_axis=0, tiled=True)


def gather(value, axes, parts):
    return exchange(jnp.broadcast_to(value, (parts, *value.shape[1:])), axes)


def on_device(token_ids, activations, grad_out, error_buffer, init_q):
    plane, near = ("x", "y"), ("core", "x", "y")
    parts, peers, depth = lax.axis_size(plane), lax.axis_size(near), lax.axis_size("z")
    replicas = depth * lax.axis_size("core")
    tokens, features = activations.shape
    width = features // parts
    columns = grad_out.shape[1]
    error_rows = error_buffer[0]
    ids = token_ids[None]
    initq_t = init_q.T

    g_all = lax.all_gather(grad_out, plane, axis=0, tiled=True)
    payload = call(
        pack_kernel,
        jax.ShapeDtypeStruct((parts, width + SPLIT_ROWS, tokens), BF16),
        [HBM] * 4,
        ids, activations, grad_out, initq_t,
        scratch=(*staged(ids, activations, grad_out, initq_t), pltpu.SemaphoreType.DMA((4,))),
        vmem=62,
    )
    recv = exchange(payload, plane)
    p_local = call(left_kernel, jax.ShapeDtypeStruct((RANK, width), F32), [VMEM] * 3, recv, error_rows, initq_t)
    p_mean = jnp.sum(gather(lax.psum(p_local, "core")[None], "z", depth), axis=0) / replicas
    p_full = gather(p_mean[None], plane, parts)
    p_own, p_again, q_terms = call(
        right_kernel,
        (
            jax.ShapeDtypeStruct((RANK, width), F32),
            jax.ShapeDtypeStruct((RANK, width), F32),
            jax.ShapeDtypeStruct((columns * RANK // LANES, LANES), F32),
        ),
        [VMEM, VMEM, HBM, HBM, HBM, VMEM],
        p_full, p_mean, ids, activations, grad_out, error_rows,
        scratch=(*staged(ids, activations, grad_out), pltpu.SemaphoreType.DMA((3,))),
    )
    blocks = exchange(q_terms.reshape(peers, 1, q_terms.size // peers), near)
    blocks = gather(jnp.sum(blocks, axis=0, keepdims=True), "z", depth)
    q_sum = gather(jnp.sum(blocks, axis=0, keepdims=True), near, peers).reshape(-1, LANES)
    error_next, q_t = final(replicas, recv, g_all, error_rows, p_again, q_sum)
    return p_own.T, q_t.T, error_next[None]


def solution(mesh):
    replicas, parts = mesh.shape["dp"], mesh.shape["fsdp"]
    side = math.isqrt(parts)
    fine = Mesh(mesh.devices.reshape(replicas // 2, 2, side, parts // side), ("z", "core", "x", "y"))
    everywhere = ("z", "core", "x", "y")
    return jax.shard_map(
        on_device,
        mesh=fine,
        in_specs=(
            P(everywhere),
            P(everywhere, None),
            P(everywhere, None),
            P(("z", "core"), ("x", "y"), None),
            P(),
        ),
        out_specs=(P(("x", "y"), None), P(), P(("z", "core"), ("x", "y"), None)),
        check_vma=False,
    )
```

```python
import functools
import math

import jax
import jax.numpy as jnp
from jax import lax
from jax.experimental import pallas as pl
from jax.experimental.pallas import tpu as pltpu
from jax.sharding import Mesh, PartitionSpec as P

RANK = 8
LANES = 128
SPLIT_ROWS = 2 * RANK
F32, BF16 = jnp.float32, jnp.bfloat16
NT = (((1,), (1,)), ((), ()))
TN = (((0,), (0,)), ((), ()))
XP_SCALE = 2.0**-8
TOKEN_CUTS = (0, 1, 3, 5, 7, 8)
COLUMN_CUTS = 2
VMEM = pl.BlockSpec(memory_space=pltpu.VMEM)
HBM = pl.BlockSpec(memory_space=pltpu.HBM)


def terms(value):
    high = value.astype(BF16).astype(F32)
    rest = value - high
    middle = rest.astype(BF16).astype(F32)
    return high, middle, rest - middle


def split(value):
    return jnp.concatenate([*terms(value), jnp.zeros_like(value)], axis=0).astype(BF16)


def join(value):
    return value[:RANK] + value[RANK : 2 * RANK] + value[2 * RANK : 3 * RANK]


def dot(a, b, dims=(((1,), (0,)), ((), ()))):
    return lax.dot_general(a, b, dims, preferred_element_type=F32)


def stack(value):
    return jnp.concatenate([value[:, i : i + LANES] for i in range(0, value.shape[1], LANES)], axis=0)


def unstack(value):
    return jnp.concatenate([value[i : i + RANK] for i in range(0, value.shape[0], RANK)], axis=1)


def lanes(ref, rows=slice(None)):
    return jnp.concatenate([ref[i, rows, :] for i in range(ref.shape[0])], axis=1)


def staged(*arrays):
    return [pltpu.VMEM(a.shape, a.dtype) for a in arrays]


def call(kernel, out_shape, specs, *args, scratch=(), vmem=40):
    nbytes = sum(math.prod(a.shape) * a.dtype.itemsize for a in args)
    return pl.pallas_call(
        kernel,
        out_shape=out_shape,
        in_specs=specs,
        out_specs=jax.tree.map(lambda _: VMEM, out_shape),
        scratch_shapes=scratch,
        compiler_params=pltpu.CompilerParams(vmem_limit_bytes=vmem * 2**20),
        cost_estimate=pl.CostEstimate(flops=0, bytes_accessed=nbytes, transcendentals=0),
    )(*args)


def pack_kernel(ids_hbm, x_hbm, g_hbm, initq_hbm, pay_ref, ids_ref, x_ref, g_ref, initq_ref, sems):
    sources = (initq_hbm, g_hbm, ids_hbm, x_hbm)
    targets = (initq_ref, g_ref, ids_ref, x_ref)
    copies = [pltpu.make_async_copy(*pair, sems.at[i]) for i, pair in enumerate(zip(sources, targets))]
    for copy in copies:
        copy.start()
    for copy in copies[:3]:
        copy.wait()
    parts, rows, _ = pay_ref.shape
    width = rows - SPLIT_ROWS
    valid = (ids_ref[...] != 1).astype(F32)
    gq = join(dot(split(initq_ref[...]), g_ref[...], NT)) * valid
    gq = jnp.concatenate(terms(gq)[:2], axis=0).astype(BF16)
    copies[3].wait()
    for i in range(parts):
        block = x_ref[:, i * width : (i + 1) * width].astype(F32).T * valid
        pay_ref[i, :width, :] = block.astype(BF16)
        pay_ref[i, width:, :] = gq


def left_kernel(recv_ref, e_ref, initq_ref, p_ref):
    width = recv_ref.shape[1] - SPLIT_ROWS
    x_cols = lanes(recv_ref, slice(0, width))
    gq = lanes(recv_ref, slice(width, None))
    p = dot(gq, x_cols, NT)
    p_ref[...] = p[:RANK] + p[RANK:] + join(dot(split(initq_ref[...]), e_ref[...], NT))


def inverse_factor(gram):
    eye = (lax.broadcasted_iota(jnp.int32, gram.shape, 0) == lax.broadcasted_iota(jnp.int32, gram.shape, 1)).astype(F32)
    row = lax.broadcasted_iota(jnp.int32, (RANK, 1), 0)
    left, right = gram, eye
    scale = jnp.zeros((RANK, 1), F32)
    for k in range(RANK):
        pivot = left[k : k + 1, k : k + 1]
        factor = jnp.where(row > k, left[:, k : k + 1] / pivot, 0.0)
        scale = jnp.where(row == k, lax.rsqrt(pivot), scale)
        next_left = left - factor * left[k : k + 1, :]
        right = right - factor * right[k : k + 1, :]
        left = next_left
    return right * scale


def right_kernel(
    pfull_ref, pown_ref, ids_hbm, x_hbm, g_hbm, e_ref, own_ref, again_ref, q_ref, ids_ref, x_ref, g_ref, sems
):
    pairs = ((ids_hbm, ids_ref), (x_hbm, x_ref), (g_hbm, g_ref))
    copies = [pltpu.make_async_copy(*pair, sems.at[i]) for i, pair in enumerate(pairs)]
    for copy in copies:
        copy.start()
    high = dict(precision=lax.Precision.HIGHEST, preferred_element_type=F32)
    p_full = lanes(pfull_ref)
    gram = lax.dot_general(p_full, p_full, NT, **high)
    inverse = inverse_factor(gram)
    factor = jnp.dot(inverse, p_full, **high)
    own = jnp.dot(inverse, pown_ref[...], **high)
    own_ref[...] = own
    again_ref[...] = own
    for copy in copies:
        copy.wait()
    valid = ids_ref[...] != 1
    xp = join(dot(split(factor * XP_SCALE), x_ref[...], NT))
    xp = split(jnp.where(valid, xp, 0.0))
    q = join(dot(xp, g_ref[...])) * (1.0 / XP_SCALE) + join(dot(split(own), e_ref[...]))
    q_ref[...] = stack(q)


def final_kernel(
    replicas, recv_ref, g_hbm, e_ref, p_ref, q_ref, out_hbm, qout_ref, g_ref, total_ref, out_ref, in_sems, out_sems
):
    width, columns = e_ref.shape
    wide = columns // COLUMN_CUTS
    cuts = [g_hbm.shape[0] * eighths // 8 for eighths in TOKEN_CUTS]
    spans = [slice(*pair) for pair in zip(cuts, cuts[1:])]
    sides = [slice(j, j + wide) for j in range(0, columns, wide)]
    loads = [pltpu.make_async_copy(g_hbm.at[s], g_ref.at[s], in_sems.at[i]) for i, s in enumerate(spans)]
    stores = [pltpu.make_async_copy(out_ref.at[:, s], out_hbm.at[:, s], out_sems.at[j]) for j, s in enumerate(sides)]
    for load in loads:
        load.start()
    q = unstack(q_ref[...]) * (1.0 / replicas)
    qout_ref[...] = q
    p_high, p_middle, p_low = terms(p_ref[...])
    q_high, q_middle, q_low = terms(q)
    p_terms = jnp.concatenate([p_high, p_high, p_middle, p_high, p_low, p_middle], axis=0).astype(BF16)
    q_terms = jnp.concatenate([q_high, q_middle, q_high, q_low, q_high, q_middle], axis=0).astype(BF16)
    for side in sides:
        total_ref[:, side] = e_ref[:, side].astype(F32) - dot(p_terms, q_terms[:, side], TN)
    x_cols = lanes(recv_ref, slice(0, width))
    for i, span in enumerate(spans):
        loads[i].wait()
        for j, side in enumerate(sides):
            total = total_ref[:, side] + dot(x_cols[:, span], g_ref[span, side])
            if i + 1 < len(spans):
                total_ref[:, side] = total
            else:
                out_ref[:, side] = total.astype(BF16)
                stores[j].start()
    for store in stores:
        store.wait()


def final(replicas, recv, g_all, error_rows, p_own, q_sum):
    width, columns = error_rows.shape
    outs = (jax.ShapeDtypeStruct((width, columns), BF16), jax.ShapeDtypeStruct((RANK, columns), F32))
    return pl.pallas_call(
        functools.partial(final_kernel, replicas),
        out_shape=outs,
        in_specs=[VMEM, HBM, VMEM, VMEM, VMEM],
        out_specs=(HBM, VMEM),
        scratch_shapes=(
            *staged(g_all),
            pltpu.VMEM(error_rows.shape, F32),
            *staged(error_rows),
            pltpu.SemaphoreType.DMA((len(TOKEN_CUTS) - 1,)),
            pltpu.SemaphoreType.DMA((COLUMN_CUTS,)),
        ),
        compiler_params=pltpu.CompilerParams(vmem_limit_bytes=48 * 2**20),
        cost_estimate=pl.CostEstimate(
            flops=2 * width * columns * g_all.shape[0],
            bytes_accessed=2 * columns * (g_all.shape[0] + 2 * width),
            transcendentals=0,
        ),
    )(recv, g_all, error_rows, p_own, q_sum)


def exchange(value, axes):
    return lax.all_to_all(value, axes, split_axis=0, concat_axis=0, tiled=True)


def gather(value, axes, parts):
    return exchange(jnp.broadcast_to(value, (parts, *value.shape[1:])), axes)


def on_device(token_ids, activations, grad_out, error_buffer, init_q):
    plane, near = ("x", "y"), ("core", "x", "y")
    parts, peers, depth = lax.axis_size(plane), lax.axis_size(near), lax.axis_size("z")
    replicas = depth * lax.axis_size("core")
    tokens, features = activations.shape
    width = features // parts
    columns = grad_out.shape[1]
    error_rows = error_buffer[0]
    ids = token_ids[None]
    initq_t = init_q.T

    g_all = lax.all_gather(grad_out, plane, axis=0, tiled=True)
    payload = call(
        pack_kernel,
        jax.ShapeDtypeStruct((parts, width + SPLIT_ROWS, tokens), BF16),
        [HBM] * 4,
        ids, activations, grad_out, initq_t,
        scratch=(*staged(ids, activations, grad_out, initq_t), pltpu.SemaphoreType.DMA((4,))),
        vmem=62,
    )
    recv = exchange(payload, plane)
    p_local = call(left_kernel, jax.ShapeDtypeStruct((RANK, width), F32), [VMEM] * 3, recv, error_rows, initq_t)
    p_mean = jnp.sum(gather(lax.psum(p_local, "core")[None], "z", depth), axis=0) / replicas
    p_full = gather(p_mean[None], plane, parts)
    p_own, p_again, q_terms = call(
        right_kernel,
        (
            jax.ShapeDtypeStruct((RANK, width), F32),
            jax.ShapeDtypeStruct((RANK, width), F32),
            jax.ShapeDtypeStruct((columns * RANK // LANES, LANES), F32),
        ),
        [VMEM, VMEM, HBM, HBM, HBM, VMEM],
        p_full, p_mean, ids, activations, grad_out, error_rows,
        scratch=(*staged(ids, activations, grad_out), pltpu.SemaphoreType.DMA((3,))),
    )
    blocks = exchange(q_terms.reshape(peers, 1, q_terms.size // peers), near)
    blocks = gather(jnp.sum(blocks, axis=0, keepdims=True), "z", depth)
    q_sum = gather(jnp.sum(blocks, axis=0, keepdims=True), near, peers).reshape(-1, LANES)
    error_next, q_t = final(replicas, recv, g_all, error_rows, p_again, q_sum)
    return p_own.T, q_t.T, error_next[None]


def solution(mesh):
    replicas, parts = mesh.shape["dp"], mesh.shape["fsdp"]
    side = math.isqrt(parts)
    fine = Mesh(mesh.devices.reshape(replicas // 2, 2, side, parts // side), ("z", "core", "x", "y"))
    everywhere = ("z", "core", "x", "y")
    return jax.shard_map(
        on_device,
        mesh=fine,
        in_specs=(
            P(everywhere),
            P(everywhere, None),
            P(everywhere, None),
            P(("z", "core"), ("x", "y"), None),
            P(),
        ),
        out_specs=(P(("x", "y"), None), P(), P(("z", "core"), ("x", "y"), None)),
        check_vma=False,
    )
```

```python
import functools
import math

import jax
import jax.numpy as jnp
from jax import lax
from jax.experimental import pallas as pl
from jax.experimental.pallas import tpu as pltpu
from jax.sharding import Mesh, PartitionSpec as P

RANK = 8
LANES = 128
SPLIT_ROWS = 2 * RANK
F32, BF16 = jnp.float32, jnp.bfloat16
NT = (((1,), (1,)), ((), ()))
TN = (((0,), (0,)), ((), ()))
XP_SCALE = 2.0**-8
TOKEN_CUTS = (0, 1, 2, 4, 6, 8, 10, 12, 14, 15, 16)
COLUMN_CUTS = 2
VMEM = pl.BlockSpec(memory_space=pltpu.VMEM)
HBM = pl.BlockSpec(memory_space=pltpu.HBM)


def terms(value):
    high = value.astype(BF16).astype(F32)
    rest = value - high
    middle = rest.astype(BF16).astype(F32)
    return high, middle, rest - middle


def split(value):
    return jnp.concatenate([*terms(value), jnp.zeros_like(value)], axis=0).astype(BF16)


def join(value):
    return value[:RANK] + value[RANK : 2 * RANK] + value[2 * RANK : 3 * RANK]


def dot(a, b, dims=(((1,), (0,)), ((), ()))):
    return lax.dot_general(a, b, dims, preferred_element_type=F32)


def stack(value):
    return jnp.concatenate([value[:, i : i + LANES] for i in range(0, value.shape[1], LANES)], axis=0)


def unstack(value):
    return jnp.concatenate([value[i : i + RANK] for i in range(0, value.shape[0], RANK)], axis=1)


def lanes(ref, rows=slice(None)):
    return jnp.concatenate([ref[i, rows, :] for i in range(ref.shape[0])], axis=1)


def staged(*arrays):
    return [pltpu.VMEM(a.shape, a.dtype) for a in arrays]


def call(kernel, out_shape, specs, *args, scratch=(), vmem=40):
    nbytes = sum(math.prod(a.shape) * a.dtype.itemsize for a in args)
    return pl.pallas_call(
        kernel,
        out_shape=out_shape,
        in_specs=specs,
        out_specs=jax.tree.map(lambda _: VMEM, out_shape),
        scratch_shapes=scratch,
        compiler_params=pltpu.CompilerParams(vmem_limit_bytes=vmem * 2**20),
        cost_estimate=pl.CostEstimate(flops=0, bytes_accessed=nbytes, transcendentals=0),
    )(*args)


def pack_kernel(ids_hbm, x_hbm, g_hbm, initq_hbm, pay_ref, ids_ref, x_ref, g_ref, initq_ref, sems):
    sources = (initq_hbm, g_hbm, ids_hbm, x_hbm)
    targets = (initq_ref, g_ref, ids_ref, x_ref)
    copies = [pltpu.make_async_copy(*pair, sems.at[i]) for i, pair in enumerate(zip(sources, targets))]
    for copy in copies:
        copy.start()
    for copy in copies[:3]:
        copy.wait()
    parts, rows, _ = pay_ref.shape
    width = rows - SPLIT_ROWS
    valid = (ids_ref[...] != 1).astype(F32)
    gq = join(dot(split(initq_ref[...]), g_ref[...], NT)) * valid
    gq = jnp.concatenate(terms(gq)[:2], axis=0).astype(BF16)
    copies[3].wait()
    for i in range(parts):
        block = x_ref[:, i * width : (i + 1) * width].astype(F32).T * valid
        pay_ref[i, :width, :] = block.astype(BF16)
        pay_ref[i, width:, :] = gq


def left_kernel(recv_ref, e_ref, initq_ref, p_ref):
    width = recv_ref.shape[1] - SPLIT_ROWS
    x_cols = lanes(recv_ref, slice(0, width))
    gq = lanes(recv_ref, slice(width, None))
    p = dot(gq, x_cols, NT)
    p_ref[...] = p[:RANK] + p[RANK:] + join(dot(split(initq_ref[...]), e_ref[...], NT))


def inverse_factor(gram):
    eye = (lax.broadcasted_iota(jnp.int32, gram.shape, 0) == lax.broadcasted_iota(jnp.int32, gram.shape, 1)).astype(F32)
    row = lax.broadcasted_iota(jnp.int32, (RANK, 1), 0)
    left, right = gram, eye
    scale = jnp.zeros((RANK, 1), F32)
    for k in range(RANK):
        pivot = left[k : k + 1, k : k + 1]
        factor = jnp.where(row > k, left[:, k : k + 1] / pivot, 0.0)
        scale = jnp.where(row == k, lax.rsqrt(pivot), scale)
        next_left = left - factor * left[k : k + 1, :]
        right = right - factor * right[k : k + 1, :]
        left = next_left
    return right * scale


def right_kernel(
    pfull_ref, pown_ref, ids_hbm, x_hbm, g_hbm, e_ref, own_ref, again_ref, q_ref, ids_ref, x_ref, g_ref, sems
):
    pairs = ((ids_hbm, ids_ref), (x_hbm, x_ref), (g_hbm, g_ref))
    copies = [pltpu.make_async_copy(*pair, sems.at[i]) for i, pair in enumerate(pairs)]
    for copy in copies:
        copy.start()
    high = dict(precision=lax.Precision.HIGHEST, preferred_element_type=F32)
    p_full = lanes(pfull_ref)
    gram = lax.dot_general(p_full, p_full, NT, **high)
    inverse = inverse_factor(gram)
    factor = jnp.dot(inverse, p_full, **high)
    own = jnp.dot(inverse, pown_ref[...], **high)
    own_ref[...] = own
    again_ref[...] = own
    for copy in copies:
        copy.wait()
    valid = ids_ref[...] != 1
    xp = join(dot(split(factor * XP_SCALE), x_ref[...], NT))
    xp = split(jnp.where(valid, xp, 0.0))
    q = join(dot(xp, g_ref[...])) * (1.0 / XP_SCALE) + join(dot(split(own), e_ref[...]))
    q_ref[...] = stack(q)


def final_kernel(
    replicas, recv_ref, g_hbm, e_ref, p_ref, q_ref, out_hbm, qout_ref, g_ref, total_ref, out_ref, in_sems, out_sems
):
    width, columns = e_ref.shape
    wide = columns // COLUMN_CUTS
    cuts = [g_hbm.shape[0] * part // 16 for part in TOKEN_CUTS]
    spans = [slice(*pair) for pair in zip(cuts, cuts[1:])]
    sides = [slice(j, j + wide) for j in range(0, columns, wide)]
    loads = [pltpu.make_async_copy(g_hbm.at[s], g_ref.at[s], in_sems.at[i]) for i, s in enumerate(spans)]
    stores = [pltpu.make_async_copy(out_ref.at[:, s], out_hbm.at[:, s], out_sems.at[j]) for j, s in enumerate(sides)]
    for load in loads:
        load.start()
    q = unstack(q_ref[...]) * (1.0 / replicas)
    qout_ref[...] = q
    p_high, p_middle, p_low = terms(p_ref[...])
    q_high, q_middle, q_low = terms(q)
    p_terms = jnp.concatenate([p_high, p_high, p_middle, p_high, p_low, p_middle], axis=0).astype(BF16)
    q_terms = jnp.concatenate([q_high, q_middle, q_high, q_low, q_high, q_middle], axis=0).astype(BF16)
    for side in sides:
        total_ref[:, side] = e_ref[:, side].astype(F32) - dot(p_terms, q_terms[:, side], TN)
    x_cols = lanes(recv_ref, slice(0, width))
    for i, span in enumerate(spans):
        loads[i].wait()
        for j, side in enumerate(sides):
            total = total_ref[:, side] + dot(x_cols[:, span], g_ref[span, side])
            if i + 1 < len(spans):
                total_ref[:, side] = total
            else:
                out_ref[:, side] = total.astype(BF16)
                stores[j].start()
    for store in stores:
        store.wait()


def final(replicas, recv, g_all, error_rows, p_own, q_sum):
    width, columns = error_rows.shape
    outs = (jax.ShapeDtypeStruct((width, columns), BF16), jax.ShapeDtypeStruct((RANK, columns), F32))
    return pl.pallas_call(
        functools.partial(final_kernel, replicas),
        out_shape=outs,
        in_specs=[VMEM, HBM, VMEM, VMEM, VMEM],
        out_specs=(HBM, VMEM),
        scratch_shapes=(
            *staged(g_all),
            pltpu.VMEM(error_rows.shape, F32),
            *staged(error_rows),
            pltpu.SemaphoreType.DMA((len(TOKEN_CUTS) - 1,)),
            pltpu.SemaphoreType.DMA((COLUMN_CUTS,)),
        ),
        compiler_params=pltpu.CompilerParams(vmem_limit_bytes=48 * 2**20),
        cost_estimate=pl.CostEstimate(
            flops=2 * width * columns * g_all.shape[0],
            bytes_accessed=2 * columns * (g_all.shape[0] + 2 * width),
            transcendentals=0,
        ),
    )(recv, g_all, error_rows, p_own, q_sum)


def exchange(value, axes):
    return lax.all_to_all(value, axes, split_axis=0, concat_axis=0, tiled=True)


def gather(value, axes, parts):
    return exchange(jnp.broadcast_to(value, (parts, *value.shape[1:])), axes)


def on_device(token_ids, activations, grad_out, error_buffer, init_q):
    plane, near = ("x", "y"), ("core", "x", "y")
    parts, peers, depth = lax.axis_size(plane), lax.axis_size(near), lax.axis_size("z")
    replicas = depth * lax.axis_size("core")
    tokens, features = activations.shape
    width = features // parts
    columns = grad_out.shape[1]
    error_rows = error_buffer[0]
    ids = token_ids[None]
    initq_t = init_q.T

    g_all = lax.all_gather(grad_out, plane, axis=0, tiled=True)
    payload = call(
        pack_kernel,
        jax.ShapeDtypeStruct((parts, width + SPLIT_ROWS, tokens), BF16),
        [HBM] * 4,
        ids, activations, grad_out, initq_t,
        scratch=(*staged(ids, activations, grad_out, initq_t), pltpu.SemaphoreType.DMA((4,))),
        vmem=62,
    )
    recv = exchange(payload, plane)
    p_local = call(left_kernel, jax.ShapeDtypeStruct((RANK, width), F32), [VMEM] * 3, recv, error_rows, initq_t)
    p_mean = jnp.sum(gather(lax.psum(p_local, "core")[None], "z", depth), axis=0) / replicas
    p_full = gather(p_mean[None], plane, parts)
    p_own, p_again, q_terms = call(
        right_kernel,
        (
            jax.ShapeDtypeStruct((RANK, width), F32),
            jax.ShapeDtypeStruct((RANK, width), F32),
            jax.ShapeDtypeStruct((columns * RANK // LANES, LANES), F32),
        ),
        [VMEM, VMEM, HBM, HBM, HBM, VMEM],
        p_full, p_mean, ids, activations, grad_out, error_rows,
        scratch=(*staged(ids, activations, grad_out), pltpu.SemaphoreType.DMA((3,))),
    )
    blocks = exchange(q_terms.reshape(peers, 1, q_terms.size // peers), near)
    blocks = gather(jnp.sum(blocks, axis=0, keepdims=True), "z", depth)
    q_sum = gather(jnp.sum(blocks, axis=0, keepdims=True), near, peers).reshape(-1, LANES)
    error_next, q_t = final(replicas, recv, g_all, error_rows, p_again, q_sum)
    return p_own.T, q_t.T, error_next[None]


def solution(mesh):
    replicas, parts = mesh.shape["dp"], mesh.shape["fsdp"]
    side = math.isqrt(parts)
    fine = Mesh(mesh.devices.reshape(replicas // 2, 2, side, parts // side), ("z", "core", "x", "y"))
    everywhere = ("z", "core", "x", "y")
    return jax.shard_map(
        on_device,
        mesh=fine,
        in_specs=(
            P(everywhere),
            P(everywhere, None),
            P(everywhere, None),
            P(("z", "core"), ("x", "y"), None),
            P(),
        ),
        out_specs=(P(("x", "y"), None), P(), P(("z", "core"), ("x", "y"), None)),
        check_vma=False,
    )
```
